32 devices in a mesh: dp: 8 (over y, x, core), tensor: 4 (over z).
Axes of the slice: x: 2, y: 2, z: 4, core: 2. Of those that a mesh axis runs over, the one named last changes fastest.
Arguments:
- tokens: bfloat16 [4096, 768], P(('dp', 'tensor')), may hold values from -6 to 6
- cotangent: bfloat16 [4096, 768], P(('dp', 'tensor')), may hold values from -6 to 6
- routes: int32 [4096, 1], P('dp'), may hold values from 0 to 3; in each aligned block of 512 rows (0 to 511, 512 to 1023, ...) at most 144 rows name the same one
- buckets: int32 [1023], replicated, may hold values from 0 to 31
- attn_gain: bfloat16 [768], P('dp'), may hold values from 0.099609375 to 1.8984375
- ffn_gain: bfloat16 [768], P('dp'), may hold values from 0.099609375 to 1.8984375
- w_query: bfloat16 [768, 768], P('dp', 'tensor'), may hold values from -0.078125 to 0.078125
- w_key: bfloat16 [768, 768], P('dp', 'tensor'), may hold values from -0.078125 to 0.078125
- w_value: bfloat16 [768, 768], P('dp', 'tensor'), may hold values from -0.21875 to 0.21875
- w_output: bfloat16 [768, 768], P('dp', 'tensor'), may hold values from -1.75 to 1.75
- rel_table: bfloat16 [12, 32], P('tensor'), may hold values from -4 to 4
- w_router: bfloat16 [768, 4], P('dp'), may hold values from -0.15625 to 0.15625
- expert_up: bfloat16 [4, 768, 3072], P(None, 'dp', 'tensor'), may hold values from -0.21875 to 0.21875
- expert_down: bfloat16 [4, 768, 3072], P(None, 'dp', 'tensor'), may hold values from -0.625 to 0.625
Outputs:
- layer_out: bfloat16 [4096, 768], P(('dp', 'tensor'))
- grad_tokens: float32 [4096, 768], P(('dp', 'tensor'))
- grad_attn_gain: float32 [768], P('dp')
- grad_ffn_gain: float32 [768], P('dp')
- grad_query: float32 [768, 768], P('dp', 'tensor')
- grad_key: float32 [768, 768], P('dp', 'tensor')
- grad_value: float32 [768, 768], P('dp', 'tensor')
- grad_output: float32 [768, 768], P('dp', 'tensor')
- grad_table: float32 [12, 32], P('tensor')
- grad_router: float32 [768, 4], P('dp')
- grad_up: float32 [4, 768, 3072], P(None, 'dp', 'tensor')
- grad_down: float32 [4, 768, 3072], P(None, 'dp', 'tensor')
The draws below stay inside these ranges and needn't reach their ends.
Inputs may be any that keep to these rules, and one draw needn't show every extreme that they name: `routes`: in each sequence (512 aligned rows, the rows of one index of dp) no expert is named by more than 144 tokens, a bound that some block reaches.
All inputs are finite; a program needn't handle non-finite values.
Results may differ from the reference program's by a relative error of at most 0.015.
Values may be sent and summed in bfloat16 or wider, within the bound.
A program may use at most 128 MiB of HBM per device.

```python
import math
import jax
import jax.numpy as jnp
import numpy as np
from jax import lax

D = 768
HEADS = 12
HEAD_DIM = 64
FF = 3072
BUCKETS = 32
EXPERTS = 4
LENGTH = 512
CAP = 144
TOKENS = 4096


def with_ends(result, key, least, largest):
    place = [jax.random.randint(jax.random.fold_in(key, axis), (), 0, length) for axis, length in enumerate(result.shape)]
    main_axis = result.shape.index(max(result.shape))
    neighbour = place[:main_axis] + [(place[main_axis] + 1) % result.shape[main_axis]] + place[main_axis + 1:]
    return result.at[tuple(place)].set(least).at[tuple(neighbour)].set(largest)


def with_spikes(result, rng, source, target, shards_of, factor):
    owner, partner = [(jnp.arange(result.shape[axis_at]) // (result.shape[axis_at] // shards_of)).reshape([-1 if axis == axis_at else 1 for axis in range(result.ndim)]) for axis_at in (source, target)]
    chosen = jax.random.permutation(rng, shards_of)[partner]
    strong = (owner == chosen) | (owner == (partner + shards_of // 2) % shards_of)
    return jnp.where(strong, factor * result, result)


def shard_levels(stream_key, extent, shards, smallest, top_value):
    level, own = 1.0, jax.random.fold_in(stream_key, 6)
    for axis_at, blocks in shards:
        draws = jnp.exp(jax.random.uniform(jax.random.fold_in(own, axis_at), (blocks,), jnp.float32, smallest / len(shards), top_value / len(shards)))
        level = level * jnp.repeat(draws, extent[axis_at] // blocks).reshape([-1 if axis == axis_at else 1 for axis in range(len(extent))])
    return level


def routed_block(stream_key, own, number, rows, number_of, top, bound, slope):
    order = jax.random.permutation(stream_key, number_of)
    crowded, usual = shares(number_of, rows * top, bound, slope, True), shares(number_of, rows * top, bound, slope, False)
    places = jnp.arange(number_of)

    def named(lengths, turn):
        used = int((lengths > 0).sum())
        fixed = max(1, used // 4)
        shifted = fixed + (places - fixed + turn * (used - fixed)) % max(1, number_of - fixed)
        return jnp.zeros((number_of,), jnp.int32).at[order[jnp.where(places < fixed, places, shifted)]].set(jnp.asarray(lengths, jnp.int32))

    lengths = jnp.where(number % 4 == 0, named(crowded, number // 4), named(usual, number - number // 4 - 1))
    mixed = jax.random.permutation(jax.random.fold_in(own, 3), number_of)
    source_of, sink = mixed[0:number_of // 2 * 2:2], mixed[1:number_of // 2 * 2:2]
    room = jnp.minimum(lengths[source_of] - 1, bound - lengths[sink]) // 2
    room = jnp.where((source_of == order[0]) | (sink == order[0]) | (lengths[sink] == 0), 0, jnp.maximum(room, 0))
    shifted = jax.random.randint(jax.random.fold_in(own, 4), (number_of // 2,), 0, 1 << 20) % (room + 1)
    lengths = lengths.at[source_of].add(-shifted).at[sink].add(shifted)
    members = jnp.searchsorted(jnp.cumsum(lengths), jnp.arange(rows * top), side="right").astype(jnp.int32)
    grid = members.reshape(top, rows).T
    grid = grid[jax.random.permutation(jax.random.fold_in(own, 1), rows)]
    turn = jax.random.randint(jax.random.fold_in(own, 2), (rows, 1), 0, top)
    return jnp.take_along_axis(grid, (jnp.arange(top)[None, :] + turn) % top, axis=1)


def shares(number_of, total, limit, skew, full):
    portions = [(1 << 20) // math.isqrt(standing ** skew) + 1 for standing in range(1, number_of + 1)]
    largest = limit if full else min(limit, max(-(-total // number_of), total * portions[0] // sum(portions)))
    least = 1 if total - largest >= number_of - 1 else 0
    given, surplus = [largest] + [least] * (number_of - 1), total - largest - least * (number_of - 1)
    while surplus > 0:
        candidates = [i for i in range(1, number_of) if given[i] < largest] or [i for i in range(1, number_of) if given[i] < limit]
        pool, budget = sum([portions[i] for i in candidates]), surplus
        for i in candidates:
            addition = min(limit - given[i], max(1, budget * portions[i] // pool), surplus)
            given[i] = given[i] + addition
            surplus = surplus - addition
    return np.array(given)


def gaussian(own_key, extent, scale, limit, shards=(), kind=jnp.bfloat16):
    result = jax.random.normal(own_key, extent, jnp.float32) * scale
    if len(shards) > 0:
        result = shard_levels(own_key, extent, shards, -0.22, 0.18) * result
    return jnp.clip(result, min=-limit, max=limit).astype(kind)


def noise_with(stream_key, dims, deviation, most, pieces, heavy, kind=jnp.bfloat16):
    drawn = deviation * jax.random.normal(stream_key, dims, jnp.float32)
    if pieces:
        drawn = drawn * shard_levels(stream_key, dims, pieces, -0.22, 0.18)
    return jnp.clip(with_spikes(drawn, jax.random.fold_in(stream_key, 3), *heavy), -most, most).astype(kind)


def setup_inputs(seed: int = 0) -> dict:
    arg_keys = jax.random.split(jax.random.key(seed), 15)
    tokens = noise_with(arg_keys[0], (TOKENS, D), 1.0, 6.0, ((0, 32),), (0, 1, 32, 2.75))
    cotangent = noise_with(arg_keys[1], (TOKENS, D), 1.0, 6.0, ((0, 32),), (0, 1, 32, 2.75))
    routes_keys = jax.random.split(jax.random.fold_in(arg_keys[2], 1), TOKENS // LENGTH)
    routes_turns = jax.random.permutation(jax.random.fold_in(arg_keys[2], 3), TOKENS // LENGTH)
    routes = jax.vmap(lambda own, number: routed_block(jax.random.fold_in(arg_keys[2], 2), own, number, LENGTH, EXPERTS, 1, CAP, 1))(routes_keys, routes_turns).reshape((TOKENS, 1))
    buckets = with_ends(jax.random.randint(arg_keys[3], (2 * LENGTH - 1,), 0, BUCKETS), jax.random.fold_in(arg_keys[3], 1), 0, BUCKETS - 1).astype(jnp.int32)
    attn_gain = jnp.clip(1.0 + 0.18 * jax.random.normal(arg_keys[4], (D,), jnp.float32), 0.099609375, 1.8984375).astype(jnp.bfloat16)
    ffn_gain = jnp.clip(1.0 + 0.18 * jax.random.normal(arg_keys[5], (D,), jnp.float32), 0.099609375, 1.8984375).astype(jnp.bfloat16)
    w_query = gaussian(arg_keys[6], (D, D), (8 * D) ** -0.5, 0.078125, ((0, 8), (1, 4)))
    w_key = gaussian(arg_keys[7], (D, D), (8 * D) ** -0.5, 0.078125, ((0, 8), (1, 4)))
    w_value = gaussian(arg_keys[8], (D, D), D ** -0.5, 0.21875, ((0, 8), (1, 4)))
    w_output = gaussian(arg_keys[9], (D, D), (max(1, 8 * D // LENGTH)) ** -0.5, 1.75, ((0, 8), (1, 4)))
    rel_table = gaussian(arg_keys[10], (HEADS, BUCKETS), 1.0, 4.0, ((0, 4),))
    w_router = gaussian(arg_keys[11], (D, EXPERTS), (2 * D) ** -0.5, 0.15625, ((0, 8),))
    expert_up = gaussian(arg_keys[12], (EXPERTS, D, FF), D ** -0.5, 0.21875, ((1, 8), (2, 4)))
    expert_down = gaussian(arg_keys[13], (EXPERTS, D, FF), (max(1, FF // 32)) ** -0.5, 0.625, ((1, 8), (2, 4)))
    return {"tokens": tokens, "cotangent": cotangent, "routes": routes, "buckets": buckets, "attn_gain": attn_gain, "ffn_gain": ffn_gain, "w_query": w_query, "w_key": w_key, "w_value": w_value, "w_output": w_output, "rel_table": rel_table, "w_router": w_router, "expert_up": expert_up, "expert_down": expert_down}


@jax.custom_vjp
def low(v):
    return lax.optimization_barrier(v.astype(jnp.bfloat16)).astype(jnp.float32)

@jax.custom_vjp
def low_back(v):
    return v

def low_keep(v):
    return (low(v), None)

def low_pass(kept, grad):
    return (grad,)

def back_keep(v):
    return (v, None)

def back_low(kept, grad):
    return (low(grad),)
low.defvjp(low_keep, low_pass)
low_back.defvjp(back_keep, back_low)
epsilon = 1e-06
highest = lax.Precision.HIGHEST

def rms_norm(tok_rows, scale_vec):
    return tok_rows * lax.rsqrt(lax.optimization_barrier(jnp.mean(tok_rows * tok_rows, axis=-1, keepdims=True)) + epsilon) * scale_vec

def slot_targets(route_ids):
    one_hot = (route_ids[:, None] == jnp.arange(EXPERTS, dtype=jnp.int32)[None, :]).astype(jnp.int32)
    before = jnp.cumsum(one_hot, axis=0) - one_hot
    slot_index = lax.optimization_barrier(jnp.sum(before * one_hot, axis=1))
    return (route_ids * CAP + slot_index).astype(jnp.int32)

def sequence_layer(seq_rows, route_ids, weights, buckets):
    attn_gain, ffn_gain, w_query, w_key, w_value, w_output, rel_table, w_router, expert_up, expert_down = weights
    length = seq_rows.shape[0]
    normed = low(rms_norm(seq_rows, attn_gain))

    def project(weight):
        return low_back(low(jnp.dot(normed, weight, precision=highest))).reshape(length, HEADS, HEAD_DIM)
    queries = project(w_query)
    key_rows = project(w_key)
    values = project(w_value)
    rel_bias = jnp.take(rel_table, buckets, axis=1)
    offsets = jnp.arange(length, dtype=jnp.int32)[None, :] - jnp.arange(length, dtype=jnp.int32)[:, None] + (length - 1)
    scores = low_back(jnp.einsum('ihd,jhd->hij', queries, key_rows, precision=highest) + jnp.take(rel_bias, offsets, axis=1))
    softmaxed = low(jax.nn.softmax(scores, axis=-1))
    context = low_back(low(jnp.einsum('hij,jhd->ihd', softmaxed, values, precision=highest))).reshape(length, D)
    attended = low_back(jnp.dot(context, w_output.T, precision=highest))
    hidden = seq_rows + attended
    normed_ffn = rms_norm(hidden, ffn_gain)
    logits = jnp.dot(normed_ffn, w_router, precision=highest)
    chosen = (route_ids[:, None] == jnp.arange(EXPERTS, dtype=jnp.int32)[None, :]).astype(jnp.float32)
    gating = lax.optimization_barrier(jnp.sum(jax.nn.softmax(logits, axis=-1) * chosen, axis=-1))
    targets = slot_targets(route_ids)
    buffer = jnp.zeros((EXPERTS * CAP, D), jnp.float32).at[targets].set(low(normed_ffn)).reshape(EXPERTS, CAP, D)
    pre_act = low_back(jnp.einsum('ecd,edf->ecf', buffer, expert_up, precision=highest))
    activated = low(jax.nn.gelu(pre_act, approximate=True))
    expert_rows = jnp.einsum('ecf,edf->ecd', activated, expert_down, precision=highest).reshape(EXPERTS * CAP, D)
    returned = low_back(expert_rows[targets])
    return hidden + gating[:, None] * returned

def reference(tokens, cotangent, routes, buckets, attn_gain, ffn_gain, w_query, w_key, w_value, w_output, rel_table, w_router, expert_up, expert_down):
    params = (attn_gain.astype(jnp.float32), ffn_gain.astype(jnp.float32), w_query.astype(jnp.float32), w_key.astype(jnp.float32), w_value.astype(jnp.float32), w_output.astype(jnp.float32), rel_table.astype(jnp.float32), w_router.astype(jnp.float32), expert_up.astype(jnp.float32), expert_down.astype(jnp.float32))
    seq_routes = routes[:, 0].reshape(-1, LENGTH)

    def forward(tok_rows, weights):

        def one_sequence(seq_pair):
            return sequence_layer(seq_pair[0], seq_pair[1], weights, buckets)
        outputs = lax.map(jax.checkpoint(one_sequence), (tok_rows.reshape(-1, LENGTH, D), seq_routes))
        return outputs.reshape(-1, D)
    layer_out, pullback = jax.vjp(forward, tokens.astype(jnp.float32), params)
    grad_tokens, grads = pullback(cotangent.astype(jnp.float32))
    return (layer_out.astype(jnp.bfloat16), grad_tokens, grads[0], grads[1], grads[2], grads[3], grads[4], grads[5], grads[6], grads[7], grads[8], grads[9])
```

```python
import math

import jax
import jax.numpy as jnp
from jax import lax
from jax.experimental import pallas as pl
from jax.experimental.pallas import tpu as pltpu
from jax.sharding import PartitionSpec as P

CAP = 144
EPS = 1e-06
HIGHEST = lax.Precision.HIGHEST
BF = jnp.bfloat16
F32 = jnp.float32
SMALL = 128
GELU_A = math.sqrt(2 / math.pi)
GELU_B = 0.044715


def dot(a, b, ca=1, cb=0, precision=None):
    return lax.dot_general(
        a, b, (((ca,), (cb,)), ((), ())), precision=precision, preferred_element_type=F32
    )


def call(kernel, outs, cost, **kw):
    return pl.pallas_call(
        kernel,
        out_shape=outs,
        compiler_params=pltpu.CompilerParams(vmem_limit_bytes=56 * 1024 * 1024),
        cost_estimate=pl.CostEstimate(flops=cost, bytes_accessed=12_000_000, transcendentals=0),
        **kw,
    )


def head_mask(shape, head, size):
    lane = lax.broadcasted_iota(jnp.int32, shape, 1)
    return (lane >= head * size) & (lane < (head + 1) * size)


def bucket_hot(buckets, count):
    ids = lax.broadcasted_iota(jnp.int32, (count, buckets.shape[1]), 0)
    return ids == buckets


def attention_forward(heads, size, tok, gain, wqkv, wout, table, buckets, na, qkv, probs, ctx, part):
    length = tok.shape[0]
    wide = 2 * length
    width = heads * size
    x = tok[...].astype(F32)
    r1 = lax.rsqrt(jnp.mean(x * x, axis=-1, keepdims=True) + EPS)
    rows = (x * r1 * gain[...]).astype(BF)
    na[...] = rows
    proj = dot(rows, wqkv[...]).astype(BF)
    qkv[...] = proj
    q, k, v = qkv[:, :width], qkv[:, width : 2 * width], qkv[:, 2 * width :]
    hot = bucket_hot(buckets[...], table.shape[1]).astype(F32).astype(BF)
    rel = dot(table[...], hot)
    row8 = lax.broadcasted_iota(jnp.int32, (8, wide), 0)
    total = jnp.zeros((length, width), F32)
    for h in range(heads):
        bias = jnp.broadcast_to(rel[h : h + 1, :], (8, wide))
        bias = pltpu.roll(bias, wide - (length - 1), 1)
        for bit in (1, 2, 4):
            bias = jnp.where((row8 & bit) != 0, pltpu.roll(bias, bit, 1), bias)
        step = 8
        while step < length:
            bias = jnp.concatenate([bias, pltpu.roll(bias, step, 1)], axis=0)
            step *= 2
        mask = head_mask(q.shape, h, size)
        scores = dot(jnp.where(mask, q, jnp.zeros_like(q)), k, 1, 1) + bias[:, :length]
        peak = jnp.max(scores, axis=-1, keepdims=True)
        ex = jnp.exp(scores - peak)
        p = ex / jnp.sum(ex, axis=-1, keepdims=True)
        probs[h] = p
        total = total + jnp.where(mask, dot(p.astype(BF), v), 0.0)
    c = total.astype(BF)
    ctx[...] = c
    part[...] = dot(c, wout[...], 1, 1).astype(BF)


def attention_backward(
    heads, size, tok, na, qkv, probs, ctx, gh, wqkv, wout, gain, buckets, gw, gout, gna, gain_grad, gtable
):
    length = tok.shape[0]
    wide = 2 * length
    width = heads * size
    q, k, v = qkv[:, :width], qkv[:, width : 2 * width], qkv[:, 2 * width :]
    g = gh[...]
    gout[...] = dot(g, ctx[...], 0, 0).astype(BF)
    gctx = dot(g, wout[...]).astype(BF)
    zero = jnp.zeros((length, width), F32)
    gq, gk, gv = zero, zero, zero
    row8 = lax.broadcasted_iota(jnp.int32, (8, wide), 0)
    diag = jnp.zeros((8, wide), F32)
    for h in range(heads):
        mask = head_mask(q.shape, h, size)
        p = probs[h]
        pb = p.astype(BF)
        dp = dot(jnp.where(mask, gctx, jnp.zeros_like(gctx)), v, 1, 1)
        inner = jnp.sum(p * dp, axis=-1, keepdims=True)
        gs = (p * (dp - inner)).astype(BF)
        gq = gq + jnp.where(mask, dot(gs, k), 0.0)
        gk = gk + jnp.where(mask, dot(gs, q, 0, 0), 0.0)
        gv = gv + jnp.where(mask, dot(pb, gctx, 0, 0), 0.0)
        t = jnp.concatenate([gs.astype(F32), jnp.zeros((length, wide - length), F32)], axis=1)
        half = length // 2
        while half >= 8:
            t = t[:half] + pltpu.roll(t[half:], wide - half, 1)
            half //= 2
        for bit in (1, 2, 4):
            t = jnp.where((row8 & bit) != 0, pltpu.roll(t, wide - bit, 1), t)
        t = jnp.sum(t, axis=0, keepdims=True)
        t = pltpu.roll(jnp.broadcast_to(t, (8, wide)), length - 1, 1)
        diag = jnp.where(row8 == h, t, diag)
    hot = bucket_hot(buckets[...], gtable.shape[1]).astype(F32)
    gtable[...] = dot(diag, hot, 1, 1, HIGHEST)
    gq, gk, gv = gq.astype(BF), gk.astype(BF), gv.astype(BF)
    rows = na[...]
    grad_na = jnp.zeros((length, tok.shape[1]), F32)
    for i, part in enumerate((gq, gk, gv)):
        gw[i] = dot(rows, part, 0, 0).astype(BF)
        grad_na = grad_na + dot(part, wqkv[:, i * width : (i + 1) * width], 1, 1)
    gna[...] = grad_na.astype(BF)
    x = tok[...].astype(F32)
    r1 = lax.rsqrt(jnp.mean(x * x, axis=-1, keepdims=True) + EPS)
    gain_grad[...] = jnp.sum(grad_na * (x * r1), axis=0, keepdims=True)


def ffn_kernel(cap, routes, rows, gating, cot, up, down, ret, gnf, gup, gdown, gret):
    e = pl.program_id(0)
    length, model = rows.shape

    @pl.when(e == 0)
    def _():
        ret[...] = jnp.zeros_like(ret)
        gnf[...] = jnp.zeros_like(gnf)
        gret[...] = (gating[...] * cot[...].astype(F32)).astype(BF)

    match = jnp.broadcast_to(routes[...] == e, (8, length))
    a = lax.broadcasted_iota(jnp.int32, (length, length), 0)
    b = lax.broadcasted_iota(jnp.int32, (length, length), 1)
    before = jnp.where(a < b, 1.0, 0.0).astype(BF)
    slot = dot(jnp.where(match, 1.0, 0.0).astype(BF), before)
    slot = jnp.where(match, slot, -1.0)[0:1, :].astype(jnp.int32)
    place = jnp.where(
        lax.broadcasted_iota(jnp.int32, (cap, length), 0) == slot, 1.0, 0.0
    ).astype(BF)
    upw, downw = up[0], down[0]
    disp = dot(place, rows[...]).astype(BF)
    gslot = dot(place, gret[...]).astype(BF)
    pre = dot(disp, upw)
    th = jnp.tanh(GELU_A * (pre + GELU_B * pre * pre * pre))
    act = (0.5 * pre * (1.0 + th)).astype(BF)
    slope = 0.5 * (1.0 + th) + 0.5 * pre * (1.0 - th * th) * GELU_A * (
        1.0 + 3.0 * GELU_B * pre * pre
    )
    gpre = (slope * dot(gslot, downw)).astype(BF)
    gdown[0] = dot(gslot, act, 0, 0).astype(BF)
    gup[0] = dot(disp, gpre, 0, 0).astype(BF)
    out = dot(act, downw, 1, 1).astype(BF)
    ret[...] += dot(place, out, 0, 0).astype(BF)
    back = dot(gpre, upw, 1, 1).astype(BF)
    gnf[...] += dot(place, back, 0, 0).astype(BF)


def per_device(
    tokens,
    cotangent,
    routes,
    buckets,
    attn_gain,
    ffn_gain,
    w_query,
    w_key,
    w_value,
    w_output,
    rel_table,
    w_router,
    expert_up,
    expert_down,
):
    local_rows, model = tokens.shape
    length = local_rows * lax.axis_size("tensor")
    heads = rel_table.shape[0]
    width = w_query.shape[1]
    size = width // heads
    experts = expert_up.shape[0]
    shard = attn_gain.shape[0]
    count = rel_table.shape[1]
    hidden_here = expert_up.shape[2]

    up_full = lax.all_gather(expert_up, "dp", axis=1, tiled=True)
    down_full = lax.all_gather(expert_down, "dp", axis=1, tiled=True)
    small = jnp.concatenate([attn_gain[:, None], ffn_gain[:, None], w_router], axis=1)
    small = jnp.pad(small, ((0, 0), (0, SMALL - small.shape[1])))
    pack = jnp.concatenate([w_query, w_key, w_value, w_output, small], axis=1)
    pack = lax.all_gather(pack, "dp", axis=0, tiled=True)
    both = lax.all_gather(
        jnp.concatenate([tokens, cotangent], axis=1), "tensor", axis=0, tiled=True
    )
    tok_all, cot_all = both[:, :model], both[:, model:]
    wqkv, wout = pack[:, : 3 * width], pack[:, 3 * width : 4 * width]
    small = pack[:, 4 * width :].astype(F32)
    gain_one = small[:, 0].reshape(1, model)
    gain_two = small[:, 1].reshape(1, model)
    router = small[:, 2 : 2 + experts]
    bucket_row = jnp.pad(buckets, (0, 2 * length - buckets.shape[0]), constant_values=-1)[None, :]
    table8 = jnp.pad(rel_table, ((0, 16 - heads), (0, 0)))

    def sds(shape, dtype=BF):
        return jax.ShapeDtypeStruct(shape, dtype)

    na, qkv, probs, ctx, part = call(
        lambda *refs: attention_forward(heads, size, *refs),
        (
            sds((length, model)),
            sds((length, 3 * width)),
            sds((heads, length, length), F32),
            sds((length, width)),
            sds((length, model)),
        ),
        3_000_000_000,
        name="attention_forward",
    )(tok_all, gain_one, wqkv, wout, table8, bucket_row)
    attended = lax.psum_scatter(part, "tensor", scatter_dimension=0, tiled=True)

    token_rows = tokens.astype(F32)
    hidden = token_rows + attended.astype(F32)
    route_all = routes[:, 0]
    route_mine = lax.dynamic_slice_in_dim(
        route_all, lax.axis_index("tensor") * local_rows, local_rows
    )
    chosen = (route_mine[:, None] == jnp.arange(experts, dtype=jnp.int32)[None, :]).astype(F32)
    r2 = lax.rsqrt(jnp.mean(hidden * hidden, axis=-1, keepdims=True) + EPS)
    u2 = hidden * r2
    nf = u2 * gain_two
    prob = jax.nn.softmax(jnp.dot(nf, router, precision=HIGHEST), axis=-1)
    gating = jnp.sum(prob * chosen, axis=-1, keepdims=True)
    gate_high = gating.astype(BF)
    gate_low = (gating - gate_high.astype(F32)).astype(BF)
    gate_cols = jnp.pad(jnp.concatenate([gate_high, gate_low], axis=1), ((0, 0), (0, SMALL - 2)))
    nf_all = lax.all_gather(
        jnp.concatenate([nf.astype(BF), gate_cols], axis=1), "tensor", axis=0, tiled=True
    )
    gate_all = jnp.sum(nf_all[:, model : model + 2].astype(F32), axis=1, keepdims=True)

    whole = lambda *shape: pl.BlockSpec(shape, lambda e: (0,) * len(shape))
    per_expert = pl.BlockSpec((1, model, hidden_here), lambda e: (e, 0, 0))
    ret, gnf, grad_up, grad_down = call(
        lambda *refs: ffn_kernel(CAP, *refs),
        (
            sds((length, model)),
            sds((length, model)),
            sds((experts, model, hidden_here)),
            sds((experts, model, hidden_here)),
        ),
        6_000_000_000,
        name="experts",
        grid=(experts,),
        in_specs=[
            whole(1, length),
            whole(length, model),
            whole(length, 1),
            whole(length, model),
            per_expert,
            per_expert,
        ],
        out_specs=[whole(length, model), whole(length, model), per_expert, per_expert],
        scratch_shapes=[pltpu.VMEM((length, model), BF)],
    )(route_all[None, :], nf_all[:, :model], gate_all, cot_all, up_full, down_full)

    traded_up = lax.all_to_all(grad_up, "dp", split_axis=1, concat_axis=0, tiled=True)
    traded_down = lax.all_to_all(grad_down, "dp", split_axis=1, concat_axis=0, tiled=True)

    summed = lax.psum_scatter(
        jnp.concatenate([ret, gnf], axis=1), "tensor", scatter_dimension=0, tiled=True
    ).astype(F32)
    returned, grad_nf = summed[:, :model], summed[:, model:]
    layer_out = (hidden + gating * returned).astype(BF)
    g = cotangent.astype(F32)
    grad_gating = jnp.sum(g * returned, axis=-1, keepdims=True)
    grad_logits = prob * (chosen - gating) * grad_gating
    grad_router = lax.dot_general(
        nf, grad_logits, (((0,), (0,)), ((), ())), precision=HIGHEST, preferred_element_type=F32
    )
    grad_n2 = grad_nf + lax.dot_general(
        grad_logits, router, (((1,), (1,)), ((), ())), precision=HIGHEST, preferred_element_type=F32
    )
    gn2 = grad_n2 * gain_two
    grad_gain_two = jnp.sum(grad_n2 * u2, axis=0)
    grad_hidden = g + r2 * (gn2 - u2 * jnp.mean(gn2 * u2, axis=-1, keepdims=True))
    gh_all = lax.all_gather(grad_hidden.astype(BF), "tensor", axis=0, tiled=True)

    gw, gout, gna, grad_gain_one, gtable = call(
        lambda *refs: attention_backward(heads, size, *refs),
        (
            sds((3, model, width)),
            sds((model, width)),
            sds((length, model)),
            sds((1, model), F32),
            sds((8, count), F32),
        ),
        4_000_000_000,
        name="attention_backward",
    )(tok_all, na, qkv, probs, ctx, gh_all, wqkv, wout, gain_one, bucket_row)
    grad_na = lax.psum_scatter(gna, "tensor", scatter_dimension=0, tiled=True).astype(F32)
    r1 = lax.rsqrt(jnp.mean(token_rows * token_rows, axis=-1, keepdims=True) + EPS)
    u1 = token_rows * r1
    gn1 = grad_na * gain_one
    grad_tokens = grad_hidden + r1 * (gn1 - u1 * jnp.mean(gn1 * u1, axis=-1, keepdims=True))

    flat_table = jnp.broadcast_to(gtable[:heads].reshape(1, heads * count), (model, heads * count))
    cols = jnp.concatenate(
        [grad_gain_one.reshape(model, 1), grad_gain_two[:, None], grad_router, flat_table], axis=1
    )
    cols = jnp.pad(cols, ((0, 0), (0, SMALL - cols.shape[1]))).astype(BF)
    summed = lax.psum_scatter(
        jnp.concatenate([gw[0], gw[1], gw[2], gout, cols], axis=1),
        "dp",
        scatter_dimension=0,
        tiled=True,
    ).astype(F32)
    grads = [summed[:, i * width : (i + 1) * width] for i in range(4)]
    smalls = summed[:, 4 * width :]
    start = 2 + experts
    grad_table = smalls[0, start : start + heads * count].reshape(heads, count)
    total = lax.psum(smalls[:, :start], "tensor")

    owners = lax.axis_size("dp")
    sum_up = jnp.sum(
        traded_up.reshape(owners, experts, shard, hidden_here).astype(F32), axis=0
    )
    sum_down = jnp.sum(
        traded_down.reshape(owners, experts, shard, hidden_here).astype(F32), axis=0
    )
    return (
        layer_out,
        grad_tokens,
        total[:, 0],
        total[:, 1],
        *grads,
        grad_table,
        total[:, 2:start],
        sum_up,
        sum_down,
    )


def solution(mesh):
    rows = P(("dp", "tensor"), None)
    square = P("dp", "tensor")
    expert = P(None, "dp", "tensor")
    in_specs = (
        rows, rows, P("dp", None), P(), P("dp"), P("dp"), square, square, square, square,
        P("tensor", None), P("dp", None), expert, expert,
    )
    out_specs = (
        rows, rows, P("dp"), P("dp"), square, square, square, square,
        P("tensor", None), P("dp", None), expert, expert,
    )
    return jax.shard_map(
        per_device, mesh=mesh, in_specs=in_specs, out_specs=out_specs, check_vma=False
    )
```

```python
import math

import jax
import jax.numpy as jnp
from jax import lax
from jax.experimental import pallas as pl
from jax.experimental.pallas import tpu as pltpu
from jax.sharding import PartitionSpec as P

CAP = 144
EPS = 1e-06
HIGHEST = lax.Precision.HIGHEST
BF = jnp.bfloat16
F32 = jnp.float32
SMALL = 128
GELU_A = math.sqrt(2 / math.pi)
GELU_B = 0.044715


def dot(a, b, ca=1, cb=0, precision=None):
    return lax.dot_general(
        a, b, (((ca,), (cb,)), ((), ())), precision=precision, preferred_element_type=F32
    )


def call(kernel, outs, cost, **kw):
    return pl.pallas_call(
        kernel,
        out_shape=outs,
        compiler_params=pltpu.CompilerParams(vmem_limit_bytes=56 * 1024 * 1024),
        cost_estimate=pl.CostEstimate(flops=cost, bytes_accessed=12_000_000, transcendentals=0),
        **kw,
    )


def head_mask(shape, head, size):
    lane = lax.broadcasted_iota(jnp.int32, shape, 1)
    return (lane >= head * size) & (lane < (head + 1) * size)


def bucket_hot(buckets, count):
    ids = lax.broadcasted_iota(jnp.int32, (count, buckets.shape[1]), 0)
    return ids == buckets


def attention_forward(heads, size, tok, gain, wqkv, wout, table, buckets, na, qkv, probs, ctx, part):
    length = tok.shape[0]
    wide = 2 * length
    width = heads * size
    x = tok[...].astype(F32)
    r1 = lax.rsqrt(jnp.mean(x * x, axis=-1, keepdims=True) + EPS)
    rows = (x * r1 * gain[...]).astype(BF)
    na[...] = rows
    proj = dot(rows, wqkv[...]).astype(BF)
    qkv[...] = proj
    q, k, v = qkv[:, :width], qkv[:, width : 2 * width], qkv[:, 2 * width :]
    hot = bucket_hot(buckets[...], table.shape[1]).astype(F32).astype(BF)
    rel = dot(table[...], hot)
    row8 = lax.broadcasted_iota(jnp.int32, (8, wide), 0)
    total = jnp.zeros((length, width), F32)
    for h in range(heads):
        bias = jnp.broadcast_to(rel[h : h + 1, :], (8, wide))
        bias = pltpu.roll(bias, wide - (length - 1), 1)
        for bit in (1, 2, 4):
            bias = jnp.where((row8 & bit) != 0, pltpu.roll(bias, bit, 1), bias)
        step = 8
        while step < length:
            bias = jnp.concatenate([bias, pltpu.roll(bias, step, 1)], axis=0)
            step *= 2
        mask = head_mask(q.shape, h, size)
        scores = dot(jnp.where(mask, q, jnp.zeros_like(q)), k, 1, 1) + bias[:, :length]
        peak = jnp.max(scores, axis=-1, keepdims=True)
        ex = jnp.exp(scores - peak)
        p = ex / jnp.sum(ex, axis=-1, keepdims=True)
        probs[h] = p
        total = total + jnp.where(mask, dot(p.astype(BF), v), 0.0)
    c = total.astype(BF)
    ctx[...] = c
    part[...] = dot(c, wout[...], 1, 1).astype(BF)


def attention_backward(
    heads, size, tok, na, qkv, probs, ctx, gh, wqkv, wout, gain, buckets, gw, gout, gna, gain_grad, gtable
):
    length = tok.shape[0]
    wide = 2 * length
    width = heads * size
    q, k, v = qkv[:, :width], qkv[:, width : 2 * width], qkv[:, 2 * width :]
    g = gh[...]
    gout[...] = dot(g, ctx[...], 0, 0).astype(BF)
    gctx = dot(g, wout[...]).astype(BF)
    zero = jnp.zeros((length, width), F32)
    gq, gk, gv = zero, zero, zero
    row8 = lax.broadcasted_iota(jnp.int32, (8, wide), 0)
    diag = jnp.zeros((8, wide), F32)
    for h in range(heads):
        mask = head_mask(q.shape, h, size)
        p = probs[h]
        pb = p.astype(BF)
        dp = dot(jnp.where(mask, gctx, jnp.zeros_like(gctx)), v, 1, 1)
        inner = jnp.sum(p * dp, axis=-1, keepdims=True)
        gs = (p * (dp - inner)).astype(BF)
        gq = gq + jnp.where(mask, dot(gs, k), 0.0)
        gk = gk + jnp.where(mask, dot(gs, q, 0, 0), 0.0)
        gv = gv + jnp.where(mask, dot(pb, gctx, 0, 0), 0.0)
        t = jnp.concatenate([gs.astype(F32), jnp.zeros((length, wide - length), F32)], axis=1)
        half = length // 2
        while half >= 8:
            t = t[:half] + pltpu.roll(t[half:], wide - half, 1)
            half //= 2
        for bit in (1, 2, 4):
            t = jnp.where((row8 & bit) != 0, pltpu.roll(t, wide - bit, 1), t)
        t = jnp.sum(t, axis=0, keepdims=True)
        t = pltpu.roll(jnp.broadcast_to(t, (8, wide)), length - 1, 1)
        diag = jnp.where(row8 == h, t, diag)
    hot = bucket_hot(buckets[...], gtable.shape[1]).astype(F32)
    gtable[...] = dot(diag, hot, 1, 1, HIGHEST)
    gq, gk, gv = gq.astype(BF), gk.astype(BF), gv.astype(BF)
    rows = na[...]
    grad_na = jnp.zeros((length, tok.shape[1]), F32)
    for i, part in enumerate((gq, gk, gv)):
        gw[i] = dot(rows, part, 0, 0).astype(BF)
        grad_na = grad_na + dot(part, wqkv[:, i * width : (i + 1) * width], 1, 1)
    gna[...] = grad_na.astype(BF)
    x = tok[...].astype(F32)
    r1 = lax.rsqrt(jnp.mean(x * x, axis=-1, keepdims=True) + EPS)
    gain_grad[...] = jnp.sum(grad_na * (x * r1), axis=0, keepdims=True)


def turn(x, k):
    n = lax.axis_size("tensor")
    return lax.ppermute(x, "tensor", [(i, (i + k) % n) for i in range(n)])


def gather_rows(x):
    n, me, rows = lax.axis_size("tensor"), lax.axis_index("tensor"), x.shape[0]
    out = jnp.zeros((n * rows, x.shape[1]), x.dtype)
    for k in range(n):
        block = x if k == 0 else turn(x, k)
        out = lax.dynamic_update_slice_in_dim(out, block, lax.rem(me + n - k, n) * rows, 0)
    return out


def scatter_rows(x):
    n, me = lax.axis_size("tensor"), lax.axis_index("tensor")
    rows = x.shape[0] // n
    total = lax.dynamic_slice_in_dim(x, me * rows, rows, 0).astype(F32)
    for k in range(1, n):
        piece = lax.dynamic_slice_in_dim(x, lax.rem(me + k, n) * rows, rows, 0)
        total = total + turn(piece, k).astype(F32)
    return total


def store_grad(grads, which, value, shard):
    if shard is None:
        grads[which, 0] = value
        return
    for o in range(grads.shape[0]):
        grads[o, which, 0] = value[o * shard : (o + 1) * shard]


def ffn_kernel(cap, shard, routes, rows, gating, cot, up, down, ret, gnf, grads, gret):
    e = pl.program_id(0)
    length, model = rows.shape

    @pl.when(e == 0)
    def _():
        ret[...] = jnp.zeros_like(ret)
        gnf[...] = jnp.zeros_like(gnf)
        gret[...] = (gating[...] * cot[...].astype(F32)).astype(BF)

    match = jnp.broadcast_to(routes[...] == e, (8, length))
    a = lax.broadcasted_iota(jnp.int32, (length, length), 0)
    b = lax.broadcasted_iota(jnp.int32, (length, length), 1)
    before = jnp.where(a < b, 1.0, 0.0).astype(BF)
    slot = dot(jnp.where(match, 1.0, 0.0).astype(BF), before)
    slot = jnp.where(match, slot, -1.0)[0:1, :].astype(jnp.int32)
    place = jnp.where(
        lax.broadcasted_iota(jnp.int32, (cap, length), 0) == slot, 1.0, 0.0
    ).astype(BF)
    upw, downw = up[0], down[0]
    disp = dot(place, rows[...]).astype(BF)
    gslot = dot(place, gret[...]).astype(BF)
    pre = dot(disp, upw)
    th = jnp.tanh(GELU_A * (pre + GELU_B * pre * pre * pre))
    act = (0.5 * pre * (1.0 + th)).astype(BF)
    slope = 0.5 * (1.0 + th) + 0.5 * pre * (1.0 - th * th) * GELU_A * (
        1.0 + 3.0 * GELU_B * pre * pre
    )
    gpre = (slope * dot(gslot, downw)).astype(BF)
    store_grad(grads, 1, dot(gslot, act, 0, 0).astype(BF), shard)
    store_grad(grads, 0, dot(disp, gpre, 0, 0).astype(BF), shard)
    out = dot(act, downw, 1, 1).astype(BF)
    ret[...] += dot(place, out, 0, 0).astype(BF)
    back = dot(gpre, upw, 1, 1).astype(BF)
    gnf[...] += dot(place, back, 0, 0).astype(BF)


def per_device(
    tokens,
    cotangent,
    routes,
    buckets,
    attn_gain,
    ffn_gain,
    w_query,
    w_key,
    w_value,
    w_output,
    rel_table,
    w_router,
    expert_up,
    expert_down,
):
    local_rows, model = tokens.shape
    length = local_rows * lax.axis_size("tensor")
    heads = rel_table.shape[0]
    width = w_query.shape[1]
    size = width // heads
    experts = expert_up.shape[0]
    shard = attn_gain.shape[0]
    count = rel_table.shape[1]
    hidden_here = expert_up.shape[2]

    up_full = lax.all_gather(expert_up, "dp", axis=1, tiled=True)
    down_full = lax.all_gather(expert_down, "dp", axis=1, tiled=True)
    small = jnp.concatenate([attn_gain[:, None], ffn_gain[:, None], w_router], axis=1)
    small = jnp.pad(small, ((0, 0), (0, SMALL - small.shape[1])))
    pack = jnp.concatenate([w_query, w_key, w_value, w_output, small], axis=1)
    pack = lax.all_gather(pack, "dp", axis=0, tiled=True)
    pack, up_full = lax.optimization_barrier((pack, up_full))
    tok_all = gather_rows(tokens)
    cot_all = gather_rows(cotangent)
    wqkv, wout = pack[:, : 3 * width], pack[:, 3 * width : 4 * width]
    small = pack[:, 4 * width :].astype(F32)
    gain_one = small[:, 0].reshape(1, model)
    gain_two = small[:, 1].reshape(1, model)
    router = small[:, 2 : 2 + experts]
    bucket_row = jnp.pad(buckets, (0, 2 * length - buckets.shape[0]), constant_values=-1)[None, :]
    table8 = jnp.pad(rel_table, ((0, 16 - heads), (0, 0)))

    def sds(shape, dtype=BF):
        return jax.ShapeDtypeStruct(shape, dtype)

    na, qkv, probs, ctx, part = call(
        lambda *refs: attention_forward(heads, size, *refs),
        (
            sds((length, model)),
            sds((length, 3 * width)),
            sds((heads, length, length), F32),
            sds((length, width)),
            sds((length, model)),
        ),
        3_000_000_000,
        name="attention_forward",
    )(tok_all, gain_one, wqkv, wout, table8, bucket_row)
    attended = scatter_rows(part)

    token_rows = tokens.astype(F32)
    hidden = token_rows + attended
    route_all = routes[:, 0]
    route_mine = lax.dynamic_slice_in_dim(
        route_all, lax.axis_index("tensor") * local_rows, local_rows
    )
    chosen = (route_mine[:, None] == jnp.arange(experts, dtype=jnp.int32)[None, :]).astype(F32)
    r2 = lax.rsqrt(jnp.mean(hidden * hidden, axis=-1, keepdims=True) + EPS)
    u2 = hidden * r2
    nf = u2 * gain_two
    prob = jax.nn.softmax(jnp.dot(nf, router, precision=HIGHEST), axis=-1)
    gating = jnp.sum(prob * chosen, axis=-1, keepdims=True)
    gate_high = gating.astype(BF)
    gate_low = (gating - gate_high.astype(F32)).astype(BF)
    gate_cols = jnp.pad(jnp.concatenate([gate_high, gate_low], axis=1), ((0, 0), (0, SMALL - 2)))
    nf_all = lax.all_gather(
        jnp.concatenate([nf.astype(BF), gate_cols], axis=1), "tensor", axis=0, tiled=True
    )
    gate_all = jnp.sum(nf_all[:, model : model + 2].astype(F32), axis=1, keepdims=True)

    whole = lambda *shape: pl.BlockSpec(shape, lambda e: (0,) * len(shape))
    per_expert = pl.BlockSpec((1, model, hidden_here), lambda e: (e, 0, 0))
    owners = lax.axis_size("dp")
    if shard % 16 == 0:
        grads_shape = (owners, 2, experts, shard, hidden_here)
        grads_spec = pl.BlockSpec((owners, 2, 1, shard, hidden_here), lambda e: (0, 0, e, 0, 0))
    else:
        grads_shape = (2, experts, model, hidden_here)
        grads_spec = pl.BlockSpec((2, 1, model, hidden_here), lambda e: (0, e, 0, 0))
    cut = shard if shard % 16 == 0 else None
    ret, gnf, grads = call(
        lambda *refs: ffn_kernel(CAP, cut, *refs),
        (
            sds((length, model)),
            sds((length, model)),
            sds(grads_shape),
        ),
        6_000_000_000,
        name="experts",
        grid=(experts,),
        in_specs=[
            whole(1, length),
            whole(length, model),
            whole(length, 1),
            whole(length, model),
            per_expert,
            per_expert,
        ],
        out_specs=[whole(length, model), whole(length, model), grads_spec],
        scratch_shapes=[pltpu.VMEM((length, model), BF)],
    )(route_all[None, :], nf_all[:, :model], gate_all, cot_all, up_full, down_full)

    if cut is None:
        grads = grads.reshape(2, experts, owners, shard, hidden_here).transpose(2, 0, 1, 3, 4)
    if owners <= 16:
        place = lax.axis_index("dp")
        traded = [lax.dynamic_index_in_dim(grads, place, 0, keepdims=False)]
        for k in range(1, owners):
            piece = lax.dynamic_index_in_dim(grads, lax.rem(place + k, owners), 0, keepdims=False)
            pairs = [(i, (i + k) % owners) for i in range(owners)]
            traded.append(lax.ppermute(piece, "dp", pairs))
    else:
        traded = lax.all_to_all(grads, "dp", split_axis=0, concat_axis=0, tiled=True)
        traded = [traded[i] for i in range(owners)]

    summed = lax.psum_scatter(
        jnp.concatenate([ret, gnf], axis=1), "tensor", scatter_dimension=0, tiled=True
    ).astype(F32)
    returned, grad_nf = summed[:, :model], summed[:, model:]
    layer_out = (hidden + gating * returned).astype(BF)
    g = cotangent.astype(F32)
    grad_gating = jnp.sum(g * returned, axis=-1, keepdims=True)
    grad_logits = prob * (chosen - gating) * grad_gating
    grad_router = lax.dot_general(
        nf, grad_logits, (((0,), (0,)), ((), ())), precision=HIGHEST, preferred_element_type=F32
    )
    grad_n2 = grad_nf + lax.dot_general(
        grad_logits, router, (((1,), (1,)), ((), ())), precision=HIGHEST, preferred_element_type=F32
    )
    gn2 = grad_n2 * gain_two
    grad_gain_two = jnp.sum(grad_n2 * u2, axis=0)
    grad_hidden = g + r2 * (gn2 - u2 * jnp.mean(gn2 * u2, axis=-1, keepdims=True))
    gh_all = lax.all_gather(grad_hidden.astype(BF), "tensor", axis=0, tiled=True)

    gw, gout, gna, grad_gain_one, gtable = call(
        lambda *refs: attention_backward(heads, size, *refs),
        (
            sds((3, model, width)),
            sds((model, width)),
            sds((length, model)),
            sds((1, model), F32),
            sds((8, count), F32),
        ),
        4_000_000_000,
        name="attention_backward",
    )(tok_all, na, qkv, probs, ctx, gh_all, wqkv, wout, gain_one, bucket_row)
    grad_na = scatter_rows(gna)
    r1 = lax.rsqrt(jnp.mean(token_rows * token_rows, axis=-1, keepdims=True) + EPS)
    u1 = token_rows * r1
    gn1 = grad_na * gain_one
    grad_tokens = grad_hidden + r1 * (gn1 - u1 * jnp.mean(gn1 * u1, axis=-1, keepdims=True))

    flat_table = jnp.broadcast_to(gtable[:heads].reshape(1, heads * count), (model, heads * count))
    cols = jnp.concatenate(
        [grad_gain_one.reshape(model, 1), grad_gain_two[:, None], grad_router, flat_table], axis=1
    )
    cols = jnp.pad(cols, ((0, 0), (0, SMALL - cols.shape[1]))).astype(BF)
    summed = lax.psum_scatter(
        jnp.concatenate([gw[0], gw[1], gw[2], gout, cols], axis=1),
        "dp",
        scatter_dimension=0,
        tiled=True,
    ).astype(F32)
    squares = [summed[:, i * width : (i + 1) * width] for i in range(4)]
    smalls = summed[:, 4 * width :]
    start = 2 + experts
    grad_table = smalls[0, start : start + heads * count].reshape(heads, count)
    mine = smalls[:, :start]
    total = mine
    for k in range(1, lax.axis_size("tensor")):
        total = total + turn(mine, k)

    sum_up = sum(part[0].astype(F32) for part in traded)
    sum_down = sum(part[1].astype(F32) for part in traded)
    return (
        layer_out,
        grad_tokens,
        total[:, 0],
        total[:, 1],
        *squares,
        grad_table,
        total[:, 2:start],
        sum_up,
        sum_down,
    )


def solution(mesh):
    rows = P(("dp", "tensor"), None)
    square = P("dp", "tensor")
    expert = P(None, "dp", "tensor")
    in_specs = (
        rows, rows, P("dp", None), P(), P("dp"), P("dp"), square, square, square, square,
        P("tensor", None), P("dp", None), expert, expert,
    )
    out_specs = (
        rows, rows, P("dp"), P("dp"), square, square, square, square,
        P("tensor", None), P("dp", None), expert, expert,
    )
    return jax.shard_map(
        per_device, mesh=mesh, in_specs=in_specs, out_specs=out_specs, check_vma=False
    )
```

```python
import math

import jax
import jax.numpy as jnp
from jax import lax
from jax.experimental import pallas as pl
from jax.experimental.pallas import tpu as pltpu
from jax.sharding import PartitionSpec as P

CAP = 144
EPS = 1e-06
HIGHEST = lax.Precision.HIGHEST
BF = jnp.bfloat16
F32 = jnp.float32
SMALL = 128
GELU_A = math.sqrt(2 / math.pi)
GELU_B = 0.044715


def dot(a, b, ca=1, cb=0, precision=None):
    return lax.dot_general(
        a, b, (((ca,), (cb,)), ((), ())), precision=precision, preferred_element_type=F32
    )


def call(kernel, outs, cost, **kw):
    return pl.pallas_call(
        kernel,
        out_shape=outs,
        compiler_params=pltpu.CompilerParams(vmem_limit_bytes=56 * 1024 * 1024),
        cost_estimate=pl.CostEstimate(flops=cost, bytes_accessed=12_000_000, transcendentals=0),
        **kw,
    )


def head_mask(shape, head, size):
    lane = lax.broadcasted_iota(jnp.int32, shape, 1)
    return (lane >= head * size) & (lane < (head + 1) * size)


def bucket_hot(buckets, count):
    ids = lax.broadcasted_iota(jnp.int32, (count, buckets.shape[1]), 0)
    return ids == buckets


def attention_forward(heads, size, tok, gain, pack, table, buckets, na, qkv, probs, ctx, part):
    length = tok.shape[0]
    wide = 2 * length
    width = heads * size
    x = tok[...].astype(F32)
    r1 = lax.rsqrt(jnp.mean(x * x, axis=-1, keepdims=True) + EPS)
    rows = (x * r1 * gain[...]).astype(BF)
    na[...] = rows
    proj = dot(rows, pack[:, : 3 * width]).astype(BF)
    qkv[...] = proj
    q, k, v = qkv[:, :width], qkv[:, width : 2 * width], qkv[:, 2 * width :]
    hot = bucket_hot(buckets[...], table.shape[1]).astype(F32).astype(BF)
    rel = dot(table[...], hot)
    row8 = lax.broadcasted_iota(jnp.int32, (8, wide), 0)
    total = jnp.zeros((length, width), F32)
    for h in range(heads):
        bias = jnp.broadcast_to(rel[h : h + 1, :], (8, wide))
        bias = pltpu.roll(bias, wide - (length - 1), 1)
        for bit in (1, 2, 4):
            bias = jnp.where((row8 & bit) != 0, pltpu.roll(bias, bit, 1), bias)
        step = 8
        while step < length:
            bias = jnp.concatenate([bias, pltpu.roll(bias, step, 1)], axis=0)
            step *= 2
        mask = head_mask(q.shape, h, size)
        scores = dot(jnp.where(mask, q, jnp.zeros_like(q)), k, 1, 1) + bias[:, :length]
        peak = jnp.max(scores, axis=-1, keepdims=True)
        ex = jnp.exp(scores - peak)
        p = ex / jnp.sum(ex, axis=-1, keepdims=True)
        probs[h] = p
        total = total + jnp.where(mask, dot(p.astype(BF), v), 0.0)
    c = total.astype(BF)
    ctx[...] = c
    part[...] = dot(c, pack[:, 3 * width : 4 * width], 1, 1).astype(BF)


def attention_backward(
    heads, size, tok, na, qkv, probs, ctx, gh, pack, gain, buckets, gw, gout, gna, gain_grad, gtable
):
    length = tok.shape[0]
    wide = 2 * length
    width = heads * size
    q, k, v = qkv[:, :width], qkv[:, width : 2 * width], qkv[:, 2 * width :]
    g = gh[...]
    gout[...] = dot(g, ctx[...], 0, 0).astype(BF)
    gctx = dot(g, pack[:, 3 * width : 4 * width]).astype(BF)
    zero = jnp.zeros((length, width), F32)
    gq, gk, gv = zero, zero, zero
    row8 = lax.broadcasted_iota(jnp.int32, (8, wide), 0)
    diag = jnp.zeros((8, wide), F32)
    for h in range(heads):
        mask = head_mask(q.shape, h, size)
        p = probs[h]
        pb = p.astype(BF)
        dp = dot(jnp.where(mask, gctx, jnp.zeros_like(gctx)), v, 1, 1)
        inner = jnp.sum(p * dp, axis=-1, keepdims=True)
        gs = (p * (dp - inner)).astype(BF)
        gq = gq + jnp.where(mask, dot(gs, k), 0.0)
        gk = gk + jnp.where(mask, dot(gs, q, 0, 0), 0.0)
        gv = gv + jnp.where(mask, dot(pb, gctx, 0, 0), 0.0)
        t = jnp.concatenate([gs.astype(F32), jnp.zeros((length, wide - length), F32)], axis=1)
        half = length // 2
        while half >= 8:
            t = t[:half] + pltpu.roll(t[half:], wide - half, 1)
            half //= 2
        for bit in (1, 2, 4):
            t = jnp.where((row8 & bit) != 0, pltpu.roll(t, wide - bit, 1), t)
        t = jnp.sum(t, axis=0, keepdims=True)
        t = pltpu.roll(jnp.broadcast_to(t, (8, wide)), length - 1, 1)
        diag = jnp.where(row8 == h, t, diag)
    hot = bucket_hot(buckets[...], gtable.shape[1]).astype(F32)
    gtable[...] = dot(diag, hot, 1, 1, HIGHEST)
    gq, gk, gv = gq.astype(BF), gk.astype(BF), gv.astype(BF)
    rows = na[...]
    grad_na = jnp.zeros((length, tok.shape[1]), F32)
    for i, part in enumerate((gq, gk, gv)):
        gw[i] = dot(rows, part, 0, 0).astype(BF)
        grad_na = grad_na + dot(part, pack[:, i * width : (i + 1) * width], 1, 1)
    gna[...] = grad_na.astype(BF)
    x = tok[...].astype(F32)
    r1 = lax.rsqrt(jnp.mean(x * x, axis=-1, keepdims=True) + EPS)
    gain_grad[...] = jnp.sum(grad_na * (x * r1), axis=0, keepdims=True)


def turn(x, k):
    n = lax.axis_size("tensor")
    return lax.ppermute(x, "tensor", [(i, (i + k) % n) for i in range(n)])


def gather_rows(x):
    n, me, rows = lax.axis_size("tensor"), lax.axis_index("tensor"), x.shape[0]
    out = jnp.zeros((n * rows, x.shape[1]), x.dtype)
    for k in range(n):
        block = x if k == 0 else turn(x, k)
        out = lax.dynamic_update_slice_in_dim(out, block, lax.rem(me + n - k, n) * rows, 0)
    return out


def scatter_rows(x):
    n, me = lax.axis_size("tensor"), lax.axis_index("tensor")
    rows = x.shape[0] // n
    total = lax.dynamic_slice_in_dim(x, me * rows, rows, 0).astype(F32)
    for k in range(1, n):
        piece = lax.dynamic_slice_in_dim(x, lax.rem(me + k, n) * rows, rows, 0)
        total = total + turn(piece, k).astype(F32)
    return total


def store_grad(grads, which, value, shard):
    if shard is None:
        grads[which, 0] = value
        return
    for o in range(grads.shape[0]):
        grads[o, which, 0] = value[o * shard : (o + 1) * shard]


def ffn_kernel(cap, shard, routes, rows, gating, cot, up, down, ret, gnf, grads, gret):
    e = pl.program_id(0)
    length, model = rows.shape

    @pl.when(e == 0)
    def _():
        ret[...] = jnp.zeros_like(ret)
        gnf[...] = jnp.zeros_like(gnf)
        gret[...] = (gating[...] * cot[...].astype(F32)).astype(BF)

    match = jnp.broadcast_to(routes[...] == e, (8, length))
    a = lax.broadcasted_iota(jnp.int32, (length, length), 0)
    b = lax.broadcasted_iota(jnp.int32, (length, length), 1)
    before = jnp.where(a < b, 1.0, 0.0).astype(BF)
    slot = dot(jnp.where(match, 1.0, 0.0).astype(BF), before)
    slot = jnp.where(match, slot, -1.0)[0:1, :].astype(jnp.int32)
    place = jnp.where(
        lax.broadcasted_iota(jnp.int32, (cap, length), 0) == slot, 1.0, 0.0
    ).astype(BF)
    upw, downw = up[0], down[0]
    disp = dot(place, rows[...]).astype(BF)
    gslot = dot(place, gret[...]).astype(BF)
    pre = dot(disp, upw)
    th = jnp.tanh(GELU_A * (pre + GELU_B * pre * pre * pre))
    act = (0.5 * pre * (1.0 + th)).astype(BF)
    slope = 0.5 * (1.0 + th) + 0.5 * pre * (1.0 - th * th) * GELU_A * (
        1.0 + 3.0 * GELU_B * pre * pre
    )
    gpre = (slope * dot(gslot, downw)).astype(BF)
    store_grad(grads, 1, dot(gslot, act, 0, 0).astype(BF), shard)
    store_grad(grads, 0, dot(disp, gpre, 0, 0).astype(BF), shard)
    out = dot(act, downw, 1, 1).astype(BF)
    ret[...] += dot(place, out, 0, 0).astype(BF)
    back = dot(gpre, upw, 1, 1).astype(BF)
    gnf[...] += dot(place, back, 0, 0).astype(BF)


def per_device(
    tokens,
    cotangent,
    routes,
    buckets,
    attn_gain,
    ffn_gain,
    w_query,
    w_key,
    w_value,
    w_output,
    rel_table,
    w_router,
    expert_up,
    expert_down,
):
    local_rows, model = tokens.shape
    length = local_rows * lax.axis_size("tensor")
    heads = rel_table.shape[0]
    width = w_query.shape[1]
    size = width // heads
    experts = expert_up.shape[0]
    shard = attn_gain.shape[0]
    count = rel_table.shape[1]
    hidden_here = expert_up.shape[2]

    up_full = lax.all_gather(expert_up, "dp", axis=1, tiled=True)
    down_full = lax.all_gather(expert_down, "dp", axis=1, tiled=True)
    small = jnp.concatenate([attn_gain[:, None], ffn_gain[:, None], w_router], axis=1)
    small = jnp.pad(small, ((0, 0), (0, SMALL - small.shape[1])))
    pack = jnp.concatenate([w_query, w_key, w_value, w_output, small], axis=1)
    pack = lax.all_gather(pack, "dp", axis=0, tiled=True)
    tok_all = gather_rows(tokens)
    cot_all = gather_rows(cotangent)
    small = pack[:, 4 * width :].astype(F32)
    gain_one = small[:, 0].reshape(1, model)
    gain_two = small[:, 1].reshape(1, model)
    router = small[:, 2 : 2 + experts]
    bucket_row = jnp.pad(buckets, (0, 2 * length - buckets.shape[0]), constant_values=-1)[None, :]
    table8 = jnp.pad(rel_table, ((0, 16 - heads), (0, 0)))

    def sds(shape, dtype=BF):
        return jax.ShapeDtypeStruct(shape, dtype)

    na, qkv, probs, ctx, part = call(
        lambda *refs: attention_forward(heads, size, *refs),
        (
            sds((length, model)),
            sds((length, 3 * width)),
            sds((heads, length, length), F32),
            sds((length, width)),
            sds((length, model)),
        ),
        3_000_000_000,
        name="attention_forward",
    )(tok_all, gain_one, pack, table8, bucket_row)
    attended = scatter_rows(part)
    attended, up_full = lax.optimization_barrier((attended, up_full))

    token_rows = tokens.astype(F32)
    hidden = token_rows + attended
    route_all = routes[:, 0]
    route_mine = lax.dynamic_slice_in_dim(
        route_all, lax.axis_index("tensor") * local_rows, local_rows
    )
    chosen = (route_mine[:, None] == jnp.arange(experts, dtype=jnp.int32)[None, :]).astype(F32)
    r2 = lax.rsqrt(jnp.mean(hidden * hidden, axis=-1, keepdims=True) + EPS)
    u2 = hidden * r2
    nf = u2 * gain_two
    prob = jax.nn.softmax(jnp.dot(nf, router, precision=HIGHEST), axis=-1)
    gating = jnp.sum(prob * chosen, axis=-1, keepdims=True)
    gate_high = gating.astype(BF)
    gate_low = (gating - gate_high.astype(F32)).astype(BF)
    gate_cols = jnp.pad(jnp.concatenate([gate_high, gate_low], axis=1), ((0, 0), (0, SMALL - 2)))
    nf_all = lax.all_gather(
        jnp.concatenate([nf.astype(BF), gate_cols], axis=1), "tensor", axis=0, tiled=True
    )
    gate_all = jnp.sum(nf_all[:, model : model + 2].astype(F32), axis=1, keepdims=True)

    whole = lambda *shape: pl.BlockSpec(shape, lambda e: (0,) * len(shape))
    per_expert = pl.BlockSpec((1, model, hidden_here), lambda e: (e, 0, 0))
    owners = lax.axis_size("dp")
    if shard % 16 == 0:
        grads_shape = (owners, 2, experts, shard, hidden_here)
        grads_spec = pl.BlockSpec((owners, 2, 1, shard, hidden_here), lambda e: (0, 0, e, 0, 0))
    else:
        grads_shape = (2, experts, model, hidden_here)
        grads_spec = pl.BlockSpec((2, 1, model, hidden_here), lambda e: (0, e, 0, 0))
    cut = shard if shard % 16 == 0 else None
    ret, gnf, grads = call(
        lambda *refs: ffn_kernel(CAP, cut, *refs),
        (
            sds((length, model)),
            sds((length, model)),
            sds(grads_shape),
        ),
        6_000_000_000,
        name="experts",
        grid=(experts,),
        in_specs=[
            whole(1, length),
            whole(length, model),
            whole(length, 1),
            whole(length, model),
            per_expert,
            per_expert,
        ],
        out_specs=[whole(length, model), whole(length, model), grads_spec],
        scratch_shapes=[pltpu.VMEM((length, model), BF)],
    )(route_all[None, :], nf_all[:, :model], gate_all, cot_all, up_full, down_full)

    if cut is None:
        grads = grads.reshape(2, experts, owners, shard, hidden_here).transpose(2, 0, 1, 3, 4)
    if owners <= 16:
        place = lax.axis_index("dp")
        traded = [lax.dynamic_index_in_dim(grads, place, 0, keepdims=False)]
        for k in range(1, owners):
            piece = lax.dynamic_index_in_dim(grads, lax.rem(place + k, owners), 0, keepdims=False)
            pairs = [(i, (i + k) % owners) for i in range(owners)]
            traded.append(lax.ppermute(piece, "dp", pairs))
    else:
        traded = lax.all_to_all(grads, "dp", split_axis=0, concat_axis=0, tiled=True)
        traded = [traded[i] for i in range(owners)]

    summed = lax.psum_scatter(
        jnp.concatenate([ret, gnf], axis=1), "tensor", scatter_dimension=0, tiled=True
    ).astype(F32)
    returned, grad_nf = summed[:, :model], summed[:, model:]
    layer_out = (hidden + gating * returned).astype(BF)
    g = cotangent.astype(F32)
    grad_gating = jnp.sum(g * returned, axis=-1, keepdims=True)
    grad_logits = prob * (chosen - gating) * grad_gating
    grad_router = lax.dot_general(
        nf, grad_logits, (((0,), (0,)), ((), ())), precision=HIGHEST, preferred_element_type=F32
    )
    grad_n2 = grad_nf + lax.dot_general(
        grad_logits, router, (((1,), (1,)), ((), ())), precision=HIGHEST, preferred_element_type=F32
    )
    gn2 = grad_n2 * gain_two
    grad_gain_two = jnp.sum(grad_n2 * u2, axis=0)
    grad_hidden = g + r2 * (gn2 - u2 * jnp.mean(gn2 * u2, axis=-1, keepdims=True))
    gh_all = lax.all_gather(grad_hidden.astype(BF), "tensor", axis=0, tiled=True)

    gw, gout, gna, grad_gain_one, gtable = call(
        lambda *refs: attention_backward(heads, size, *refs),
        (
            sds((3, model, width)),
            sds((model, width)),
            sds((length, model)),
            sds((1, model), F32),
            sds((8, count), F32),
        ),
        4_000_000_000,
        name="attention_backward",
    )(tok_all, na, qkv, probs, ctx, gh_all, pack, gain_one, bucket_row)
    grad_na = scatter_rows(gna)
    r1 = lax.rsqrt(jnp.mean(token_rows * token_rows, axis=-1, keepdims=True) + EPS)
    u1 = token_rows * r1
    gn1 = grad_na * gain_one
    grad_tokens = grad_hidden + r1 * (gn1 - u1 * jnp.mean(gn1 * u1, axis=-1, keepdims=True))

    flat_table = jnp.broadcast_to(gtable[:heads].reshape(1, heads * count), (model, heads * count))
    cols = jnp.concatenate(
        [grad_gain_one.reshape(model, 1), grad_gain_two[:, None], grad_router, flat_table], axis=1
    )
    cols = jnp.pad(cols, ((0, 0), (0, SMALL - cols.shape[1]))).astype(BF)
    summed = lax.psum_scatter(
        jnp.concatenate([gw[0], gw[1], gw[2], gout, cols], axis=1),
        "dp",
        scatter_dimension=0,
        tiled=True,
    ).astype(F32)
    squares = [summed[:, i * width : (i + 1) * width] for i in range(4)]
    smalls = summed[:, 4 * width :]
    start = 2 + experts
    grad_table = smalls[0, start : start + heads * count].reshape(heads, count)
    mine = smalls[:, :start]
    total = mine
    for k in range(1, lax.axis_size("tensor")):
        total = total + turn(mine, k)

    sum_up = sum(part[0].astype(F32) for part in traded)
    sum_down = sum(part[1].astype(F32) for part in traded)
    return (
        layer_out,
        grad_tokens,
        total[:, 0],
        total[:, 1],
        *squares,
        grad_table,
        total[:, 2:start],
        sum_up,
        sum_down,
    )


def solution(mesh):
    rows = P(("dp", "tensor"), None)
    square = P("dp", "tensor")
    expert = P(None, "dp", "tensor")
    in_specs = (
        rows, rows, P("dp", None), P(), P("dp"), P("dp"), square, square, square, square,
        P("tensor", None), P("dp", None), expert, expert,
    )
    out_specs = (
        rows, rows, P("dp"), P("dp"), square, square, square, square,
        P("tensor", None), P("dp", None), expert, expert,
    )
    return jax.shard_map(
        per_device, mesh=mesh, in_specs=in_specs, out_specs=out_specs, check_vma=False
    )
```
